32 devices in a mesh: grp: 2 (over y), ha: 4 (over z), wa: 4 (over x, core).
Axes of the slice: x: 2, y: 2, z: 4, core: 2. Of those that a mesh axis runs over, the one named last changes fastest.
Arguments:
- inputs: bfloat16 [8, 16, 64, 128], P('grp', 'ha', 'wa'), parts along dimension 0, may hold values from -40 to 40
- upstream: bfloat16 [8, 16, 64, 128], P('grp', 'ha', 'wa'), parts along dimension 0, may hold values from -40 to 40
- kernels: bfloat16 [4, 3456, 128], replicated, may hold values from -0.109375 to 0.109375
- norm_gain: float32 [4, 128], replicated, may hold values from 0.1 to 1.9
- norm_shift: float32 [4, 128], replicated, may hold values from -3 to 3
Outputs:
- input_grad: bfloat16 [8, 16, 64, 128], P('grp', 'ha', 'wa'), parts along dimension 0
- kernel_grads: float32 [8, 27, 16384], P('grp', None, ('ha', 'wa')), parts along dimension 0
- norm_grads: float32 [4, 4, 128], P('grp'), parts along dimension 0
The draws below stay inside these ranges and needn't reach their ends.
There are 2 independent parts, one for each index of `grp`. The reference program is written for one: setup_inputs(seed, part) draws one part's arguments, and reference() takes and returns one part's arrays. A program takes and returns all parts, laid end to end along the dimension named above; an argument that names none is the same for every part. Nothing has to cross between parts.
All inputs are finite; a program needn't handle non-finite values.
Results may differ from the reference program's by a relative error of at most 0.0059.
Values may be sent and summed in bfloat16 or wider, within the bound.
A program may use at most 64 MiB of HBM per device.

```python
import math
import jax
import jax.numpy as jnp
from jax import lax

C = 128
F = 4
BLOCKS = 2
NH = 16
NW = 64


def scale_ramp(key, count):
    exponent = 0.5 * jnp.arange(count, dtype=jnp.float32) / count + 0.5 * jax.random.uniform(key, (count,), jnp.float32)
    return jnp.exp(jnp.log(10.0) * exponent)


def field_draw(keys, factor):
    base = jnp.clip(jax.random.normal(keys[0], (F, NH, NW, C), jnp.float32), -4.0, 4.0)
    rows = scale_ramp(keys[1], NH)[None, :, None, None]
    columns = scale_ramp(keys[2], NW)[None, None, :, None]
    return (base * rows * columns * factor).astype(jnp.bfloat16)


def draw_inputs(key, part):
    key = jax.random.fold_in(key, 3)
    return field_draw(jax.random.split(key, 4), 0.1)


def draw_upstream(key, part):
    key = jax.random.fold_in(key, 7)
    return field_draw(jax.random.split(key, 4), 0.1)


def scatter_about(stream_key, shape, deviation, bound, kind=jnp.bfloat16):
    entries = jax.random.normal(stream_key, shape, jnp.float32) * deviation
    return jnp.minimum(jnp.maximum(entries, -bound), bound).astype(kind)


def setup_inputs(seed: int = 0, part: int = 0) -> dict:
    arg_keys = jax.random.split(jax.random.key(seed), 6)
    part_keys = jax.random.split(jax.random.fold_in(arg_keys[5], part), 6)
    inputs = draw_inputs(jax.random.fold_in(jax.random.fold_in(arg_keys[5], part), 71), part)
    upstream = draw_upstream(jax.random.fold_in(jax.random.fold_in(arg_keys[5], part), 71), part)
    kernels = scatter_about(arg_keys[2], (2 * BLOCKS, 27 * C, C), (27 * C) ** -0.5, 0.109375)
    norm_gain = jnp.clip(1.0 + 0.18 * jax.random.normal(arg_keys[3], (2 * BLOCKS, C), jnp.float32), 0.1, 1.9)
    norm_shift = scatter_about(arg_keys[4], (2 * BLOCKS, C), 0.5, 3.0, jnp.float32)
    return dict(inputs=inputs, upstream=upstream, kernels=kernels, norm_gain=norm_gain, norm_shift=norm_shift)


norm_eps = 1e-06

def time_pad(values):
    return jnp.concatenate([values[:1], values[:1], values], axis=0)

def padded_acts(acts):
    return jnp.pad(time_pad(acts.astype(jnp.float32)), ((0, 0), (1, 1), (1, 1), (0, 0)))

def conv_whole(acts, kernel):
    chans = acts.shape[-1]
    weights = kernel.astype(jnp.float32).reshape(3, 3, 3, chans, chans)
    return lax.conv_general_dilated(padded_acts(acts)[None], weights, (1, 1, 1), 'VALID', dimension_numbers=('NDHWC', 'DHWIO', 'NDHWC'), precision=lax.Precision.HIGHEST)[0]

def conv_back_whole(grads, kernel):
    chans = grads.shape[-1]
    padded = jnp.pad(grads.astype(jnp.float32), ((2, 2), (1, 1), (1, 1), (0, 0)))
    weights = jnp.flip(kernel.astype(jnp.float32).reshape(3, 3, 3, chans, chans), (0, 1, 2)).swapaxes(3, 4)
    spread_back = lax.conv_general_dilated(padded[None], weights, (1, 1, 1), 'VALID', dimension_numbers=('NDHWC', 'DHWIO', 'NDHWC'), precision=lax.Precision.HIGHEST)[0]
    return jnp.concatenate([spread_back[0:1] + spread_back[1:2] + spread_back[2:3], spread_back[3:]], axis=0)

def kernel_whole(acts, grads):
    chans = acts.shape[-1]
    padded = padded_acts(acts)
    flat_grads = grads.astype(jnp.float32).reshape(-1, chans)
    terms = []
    for tap_t in range(3):
        for tap_h in range(3):
            for tap_w in range(3):
                piece = padded[tap_t:tap_t + F, tap_h:tap_h + NH, tap_w:tap_w + NW].reshape(-1, chans)
                terms.append(lax.dot_general(piece, flat_grads, (((0,), (0,)), ((), ())), precision=lax.Precision.HIGHEST))
    return jnp.stack(terms).reshape(27, chans * chans)

def norm_whole(values, gain, shift):
    count = NH * NW * C
    frame_mean = lax.optimization_barrier(jnp.sum(values, axis=(1, 2, 3))) / count
    centered = values - frame_mean[:, None, None, None]
    frame_var = lax.optimization_barrier(jnp.sum(centered * centered, axis=(1, 2, 3))) / count
    inv_std = lax.rsqrt(frame_var + norm_eps)
    normed = centered * inv_std[:, None, None, None]
    return (normed, inv_std, normed * gain + shift)

def silu_slope(pre):
    sigmoid_pre = jax.nn.sigmoid(pre)
    return sigmoid_pre * (1.0 + pre * (1.0 - sigmoid_pre))

def norm_back_whole(slope_grad, normed, inv_std, gain):
    count = NH * NW * C
    weighted = slope_grad * gain
    sum_w = lax.optimization_barrier(jnp.sum(weighted, axis=(1, 2, 3)))
    sum_wx = lax.optimization_barrier(jnp.sum(weighted * normed, axis=(1, 2, 3)))
    into = inv_std[:, None, None, None] * (weighted - sum_w[:, None, None, None] / count - normed * sum_wx[:, None, None, None] / count)
    return (into, lax.optimization_barrier(jnp.sum(slope_grad * normed, axis=(0, 1, 2))), lax.optimization_barrier(jnp.sum(slope_grad, axis=(0, 1, 2))))

def reference(inputs, upstream, kernels, norm_gain, norm_shift):
    stream = inputs.astype(jnp.float32)
    saved = []
    for block_id in range(BLOCKS):
        first = 2 * block_id
        second = first + 1
        normed_a, inv_a, pre_a = norm_whole(stream, norm_gain[first], norm_shift[first])
        acts_a = jax.nn.silu(pre_a).astype(jnp.bfloat16)
        conv_a = conv_whole(acts_a, kernels[first])
        normed_b, inv_b, pre_b = norm_whole(conv_a, norm_gain[second], norm_shift[second])
        acts_b = jax.nn.silu(pre_b).astype(jnp.bfloat16)
        stream = stream + conv_whole(acts_b, kernels[second])
        saved.append((normed_a, inv_a, pre_a, acts_a, normed_b, inv_b, pre_b, acts_b))
    grad_stream = upstream.astype(jnp.float32)
    kernel_terms = [None] * (2 * BLOCKS)
    gain_parts = [None] * (2 * BLOCKS)
    shift_parts = [None] * (2 * BLOCKS)
    for block_id in reversed(range(BLOCKS)):
        first = 2 * block_id
        second = first + 1
        normed_a, inv_a, pre_a, acts_a, normed_b, inv_b, pre_b, acts_b = saved[block_id]
        out_b = grad_stream.astype(jnp.bfloat16)
        kernel_terms[second] = kernel_whole(acts_b, out_b)
        slope_b = conv_back_whole(out_b, kernels[second]) * silu_slope(pre_b)
        into_b, gain_parts[second], shift_parts[second] = norm_back_whole(slope_b, normed_b, inv_b, norm_gain[second])
        out_a = into_b.astype(jnp.bfloat16)
        kernel_terms[first] = kernel_whole(acts_a, out_a)
        slope_a = conv_back_whole(out_a, kernels[first]) * silu_slope(pre_a)
        into_a, gain_parts[first], shift_parts[first] = norm_back_whole(slope_a, normed_a, inv_a, norm_gain[first])
        grad_stream = grad_stream + into_a
    scale = 1.0 / math.sqrt(F * NH * NW)
    kernel_grads = jnp.stack(kernel_terms) * scale
    norm_grads = jnp.stack([jnp.stack(gain_parts), jnp.stack(shift_parts)]) * scale
    return (grad_stream.astype(jnp.bfloat16), kernel_grads, norm_grads)
```

```python
import math

import jax
import jax.numpy as jnp
from jax import lax
from jax.experimental import pallas as pl
from jax.experimental.pallas import tpu as pltpu
from jax.sharding import PartitionSpec as P

norm_eps = 1e-06
MESH = pl.DeviceIdType.MESH


def exchange_kernel(stat, edges, all_stat, border, stat_send, stat_recv, edge_send, edge_recv, *, rows_n, cols_n, pieces):
    n = rows_n * cols_n
    g, a, w = lax.axis_index("grp"), lax.axis_index("ha"), lax.axis_index("wa")
    me = a * cols_n + w
    border[...] = jnp.zeros_like(border)
    barrier = pltpu.get_barrier_semaphore()

    def device(index):
        return (g, lax.div(index, cols_n), lax.rem(index, cols_n))

    for k in range(1, n):
        pl.semaphore_signal(barrier, inc=1, device_id=device(lax.rem(me + k, n)), device_id_type=MESH)
    pl.semaphore_wait(barrier, n - 1)
    plans = []
    for i, (dh, dw, src, dst, size) in enumerate(pieces):
        ok_to = (a + dh >= 0) & (a + dh < rows_n) & (w + dw >= 0) & (w + dw < cols_n)
        ok_from = (a - dh >= 0) & (a - dh < rows_n) & (w - dw >= 0) & (w - dw < cols_n)
        copy = pltpu.make_async_remote_copy(
            edges.at[pl.ds(src, size)],
            border.at[pl.ds(dst, size)],
            edge_send.at[i],
            edge_recv.at[i],
            device_id=(g, a + dh, w + dw),
            device_id_type=MESH,
        )
        plans.append((ok_to, ok_from, copy))

        @pl.when(ok_to)
        def _():
            copy.start()

    all_stat[0] = stat[...]
    copies = []
    for k in range(1, n):
        copy = pltpu.make_async_remote_copy(
            stat,
            all_stat.at[k],
            stat_send.at[k],
            stat_recv.at[k],
            device_id=device(lax.rem(me + k, n)),
            device_id_type=MESH,
        )
        copy.start()
        copies.append(copy)
    for copy in copies:
        copy.wait()
    for ok_to, ok_from, copy in plans:

        @pl.when(ok_to)
        def _():
            copy.wait_send()

        @pl.when(ok_from)
        def _():
            copy.wait_recv()


def exchange(stat, values, rows_n, cols_n):
    frames, rows, width, chans = values.shape
    lines = [
        (-1, 0, values[:, 0]),
        (1, 0, values[:, -1]),
        (0, -1, values[:, :, 0]),
        (0, 1, values[:, :, -1]),
    ]
    corner = []
    for dh in (-1, 1):
        for dw in (-1, 1):
            piece = values[:, 0 if dh < 0 else -1, 0 if dw < 0 else -1]
            corner.append((dh, dw, jnp.pad(piece, ((0, -frames % 8), (0, 0)))))
    parts, pieces, offset = [], [], 0
    where = {}
    for dh, dw, piece in lines + corner:
        flat = piece.reshape(-1, chans)
        pieces.append((dh, dw, offset, offset, flat.shape[0]))
        where[dh, dw] = (offset, flat.shape[0])
        parts.append(flat)
        offset += flat.shape[0]
    packed = jnp.concatenate(parts, axis=0)
    n = rows_n * cols_n
    vmem = pl.BlockSpec(memory_space=pltpu.VMEM)

    def run(*args, **kw):
        return exchange_kernel(*args, rows_n=rows_n, cols_n=cols_n, pieces=pieces, **kw)

    all_stat, border = pl.pallas_call(
        run,
        out_shape=(
            jax.ShapeDtypeStruct((n,) + stat.shape, jnp.float32),
            jax.ShapeDtypeStruct(packed.shape, jnp.float32),
        ),
        in_specs=[vmem, vmem],
        out_specs=(vmem, vmem),
        scratch_shapes=[
            pltpu.SemaphoreType.DMA((n,)),
            pltpu.SemaphoreType.DMA((n,)),
            pltpu.SemaphoreType.DMA((8,)),
            pltpu.SemaphoreType.DMA((8,)),
        ],
        compiler_params=pltpu.CompilerParams(collective_id=0, has_side_effects=True),
    )(stat, packed)

    def got(dh, dw, shape):
        start, size = where[dh, dw]
        return border[start : start + math.prod(shape[:-1])].reshape(shape)

    below = got(-1, 0, (frames, 1, width, chans))
    above = got(1, 0, (frames, 1, width, chans))
    after = got(0, -1, (frames, rows, 1, chans))
    before = got(0, 1, (frames, rows, 1, chans))
    one = (frames, 1, 1, chans)
    top = jnp.concatenate([got(1, 1, one), above, got(1, -1, one)], axis=2)
    mid = jnp.concatenate([before, values, after], axis=2)
    low = jnp.concatenate([got(-1, 1, one), below, got(-1, -1, one)], axis=2)
    return all_stat, jnp.concatenate([top, mid, low], axis=1)


def tap_patches(padded, frames, rows, width):
    pieces = []
    for tap_t in range(3):
        for tap_h in range(3):
            for tap_w in range(3):
                pieces.append(padded[tap_t : tap_t + frames, tap_h : tap_h + rows, tap_w : tap_w + width])
    joined = jnp.concatenate(pieces, axis=-1)
    return joined.reshape(frames * rows * width, joined.shape[-1])


def act_patches(acts):
    frames, rows, width, _ = acts.shape
    padded = jnp.concatenate([acts[:1], acts[:1], acts], axis=0)
    return tap_patches(padded, frames, rows - 2, width - 2)


def conv_backward(grads, flipped):
    frames, rows, width, chans = grads.shape
    rows, width = rows - 2, width - 2
    padded = jnp.pad(grads, ((2, 2), (0, 0), (0, 0), (0, 0)))
    patches = tap_patches(padded, frames + 2, rows, width)
    back = jnp.dot(patches, flipped, preferred_element_type=jnp.float32).reshape(frames + 2, rows, width, chans)
    return jnp.concatenate([back[0:1] + back[1:2] + back[2:3], back[3:]], axis=0)


def flip_kernel(kernel, chans):
    shaped = kernel.reshape(3, 3, 3, chans, chans)
    return jnp.flip(shaped, (0, 1, 2)).swapaxes(3, 4).reshape(27 * chans, chans)


def silu_slope(pre):
    sigmoid_pre = jax.nn.sigmoid(pre)
    return sigmoid_pre * (1.0 + pre * (1.0 - sigmoid_pre))


def interior(x):
    return x[:, 1:-1, 1:-1]


def body(inputs, upstream, kernels, norm_gain, norm_shift):
    frames, rows, width, chans = inputs.shape
    rows_n, cols_n = lax.axis_size("ha"), lax.axis_size("wa")
    total_rows, total_width = rows * rows_n, width * cols_n
    count = total_rows * total_width * chans
    local = rows * width
    scale = 1.0 / math.sqrt(frames * total_rows * total_width)
    layers = kernels.shape[0]
    a, w = lax.axis_index("ha"), lax.axis_index("wa")
    row_id = a * rows - 1 + jnp.arange(rows + 2)
    col_id = w * width - 1 + jnp.arange(width + 2)
    inside = ((row_id >= 0) & (row_id < total_rows))[:, None] & ((col_id >= 0) & (col_id < total_width))[None]
    inside = inside[None, :, :, None]

    def norm_forward(values, layer):
        sums = jnp.sum(values, axis=(1, 2))
        centred = values - (sums / local)[:, None, None]
        stat = jnp.concatenate([sums, jnp.sum(centred * centred, axis=(1, 2))], axis=0)
        all_stat, bordered = exchange(stat, values, rows_n, cols_n)
        all_sums, all_squares = all_stat[:, :frames], all_stat[:, frames:]
        mean = jnp.sum(all_sums, axis=(0, 2)) / count
        gap = all_sums / local - mean[None, :, None]
        var = jnp.sum(all_squares + local * gap * gap, axis=(0, 2)) / count
        inv_std = lax.rsqrt(var + norm_eps)
        normed = (bordered - mean[:, None, None, None]) * inv_std[:, None, None, None]
        pre = normed * norm_gain[layer] + norm_shift[layer]
        acts = jnp.where(inside, jax.nn.silu(pre), 0.0).astype(jnp.bfloat16)
        return normed, inv_std, pre, act_patches(acts), bordered

    def conv(patches, layer):
        return jnp.dot(patches, kernels[layer], preferred_element_type=jnp.float32).reshape(frames, rows, width, chans)

    terms, gains, shifts = [None] * layers, [None] * layers, [None] * layers
    stream = inputs.astype(jnp.float32)
    saved = []
    for layer in range(layers):
        if layer % 2 == 0:
            state = norm_forward(stream, layer)
        else:
            state = norm_forward(conv(saved[-1][3], layer - 1), layer)
            if layer < layers - 1:
                stream = stream + conv(state[3], layer)
        saved.append(state)

    def step_back(out, layer):
        normed, inv_std, pre, patches, _ = saved[layer]
        flat = interior(out).reshape(-1, chans)
        term = lax.dot_general(patches, flat, (((0,), (0,)), ((), ())), preferred_element_type=jnp.float32)
        terms[layer] = term.reshape(27, chans * chans)
        dn = conv_backward(out, flip_kernel(kernels[layer], chans)) * silu_slope(interior(pre))
        stat = jnp.concatenate([jnp.sum(dn, axis=(1, 2)), jnp.sum(dn * interior(normed), axis=(1, 2))], axis=0)
        all_stat, bordered = exchange(stat, dn, rows_n, cols_n)
        total = jnp.sum(all_stat, axis=0)
        shifts[layer] = jnp.sum(total[:frames], axis=0)
        gains[layer] = jnp.sum(total[frames:], axis=0)
        gain = norm_gain[layer]
        s1 = (jnp.sum(total[:frames] * gain, axis=1) / count)[:, None, None, None]
        s2 = (jnp.sum(total[frames:] * gain, axis=1) / count)[:, None, None, None]
        into = inv_std[:, None, None, None] * (bordered * gain - s1 - normed * s2)
        return jnp.where(inside, into, 0.0)

    up = upstream.astype(jnp.float32)
    _, grad_stream = exchange(jnp.zeros((2 * frames, chans), jnp.float32), up, rows_n, cols_n)
    for layer in range(layers - 1, 0, -2):
        out_a = step_back(grad_stream.astype(jnp.bfloat16), layer).astype(jnp.bfloat16)
        grad_stream = grad_stream + step_back(out_a, layer - 1)
    stacked = lax.psum_scatter(jnp.stack(terms), ("ha", "wa"), scatter_dimension=2, tiled=True)
    norm_grads = jnp.stack([jnp.stack(gains), jnp.stack(shifts)]) * scale
    return (interior(grad_stream).astype(jnp.bfloat16), stacked * scale, norm_grads)


def solution(mesh):
    return jax.shard_map(
        body,
        mesh=mesh,
        in_specs=(P("grp", "ha", "wa", None), P("grp", "ha", "wa", None), P(), P(), P()),
        out_specs=(P("grp", "ha", "wa", None), P("grp", None, ("ha", "wa")), P("grp", None, None)),
        check_vma=False,
    )
```

```python
import math

import jax
import jax.numpy as jnp
from jax import lax
from jax.experimental import pallas as pl
from jax.experimental.pallas import tpu as pltpu
from jax.sharding import PartitionSpec as P

norm_eps = 1e-06
MESH = pl.DeviceIdType.MESH


def exchange_kernel(stat, edges, all_stat, border, stat_send, stat_recv, edge_send, edge_recv, *, rows_n, cols_n, pieces):
    n = rows_n * cols_n
    g, a, w = lax.axis_index("grp"), lax.axis_index("ha"), lax.axis_index("wa")
    me = a * cols_n + w
    border[...] = jnp.zeros_like(border)
    barrier = pltpu.get_barrier_semaphore()

    def device(index):
        return (g, lax.div(index, cols_n), lax.rem(index, cols_n))

    for k in range(1, n):
        pl.semaphore_signal(barrier, inc=1, device_id=device(lax.rem(me + k, n)), device_id_type=MESH)
    pl.semaphore_wait(barrier, n - 1)
    plans = []
    for i, (dh, dw, src, dst, size) in enumerate(pieces):
        ok_to = (a + dh >= 0) & (a + dh < rows_n) & (w + dw >= 0) & (w + dw < cols_n)
        ok_from = (a - dh >= 0) & (a - dh < rows_n) & (w - dw >= 0) & (w - dw < cols_n)
        copy = pltpu.make_async_remote_copy(
            edges.at[pl.ds(src, size)],
            border.at[pl.ds(dst, size)],
            edge_send.at[i],
            edge_recv.at[i],
            device_id=(g, a + dh, w + dw),
            device_id_type=MESH,
        )
        plans.append((ok_to, ok_from, copy))

        @pl.when(ok_to)
        def _():
            copy.start()

    all_stat[0] = stat[...]
    copies = []
    for k in range(1, n):
        copy = pltpu.make_async_remote_copy(
            stat,
            all_stat.at[k],
            stat_send.at[k],
            stat_recv.at[k],
            device_id=device(lax.rem(me + k, n)),
            device_id_type=MESH,
        )
        copy.start()
        copies.append(copy)
    for copy in copies:
        copy.wait()
    for ok_to, ok_from, copy in plans:

        @pl.when(ok_to)
        def _():
            copy.wait_send()

        @pl.when(ok_from)
        def _():
            copy.wait_recv()


def border_plan(frames, rows, width):
    moves = [(-1, 0, frames * width), (1, 0, frames * width), (0, -1, frames * rows), (0, 1, frames * rows)]
    moves += [(dh, dw, 8 * pl.cdiv(frames, 8)) for dh in (-1, 1) for dw in (-1, 1)]
    plan, offset = {}, 0
    for dh, dw, size in moves:
        plan[dh, dw] = (offset, size)
        offset += size
    return plan, offset


def exchange(stat, packed, plan, rows_n, cols_n):
    pieces = [(dh, dw, start, start, size) for (dh, dw), (start, size) in plan.items()]
    n = rows_n * cols_n
    vmem = pl.BlockSpec(memory_space=pltpu.VMEM)

    def run(*args):
        return exchange_kernel(*args, rows_n=rows_n, cols_n=cols_n, pieces=pieces)

    return pl.pallas_call(
        run,
        out_shape=(
            jax.ShapeDtypeStruct((n,) + stat.shape, jnp.float32),
            jax.ShapeDtypeStruct(packed.shape, jnp.float32),
        ),
        in_specs=[vmem, vmem],
        out_specs=(vmem, vmem),
        scratch_shapes=[
            pltpu.SemaphoreType.DMA((n,)),
            pltpu.SemaphoreType.DMA((n,)),
            pltpu.SemaphoreType.DMA((8,)),
            pltpu.SemaphoreType.DMA((8,)),
        ],
        compiler_params=pltpu.CompilerParams(collective_id=0, has_side_effects=True),
    )(stat, packed)


def pack(edges, values, plan):
    frames, rows, width, chans = values.shape
    for (dh, dw), (start, size) in plan.items():
        row = 0 if dh < 0 else rows - 1
        col = 0 if dw < 0 else width - 1
        for f in range(frames):
            if dw == 0:
                edges[pl.ds(start + f * width, width), :] = values[f, row]
            elif dh == 0:
                for r in range(rows):
                    edges[pl.ds(start + f * rows + r, 1), :] = values[f, r, pl.ds(col, 1), :]
            else:
                edges[pl.ds(start + f, 1), :] = values[f, row, pl.ds(col, 1), :]
        if dh != 0 and dw != 0 and size > frames:
            edges[pl.ds(start + frames, size - frames), :] = jnp.zeros((size - frames, chans), jnp.float32)


def unpack(wide, values, border, plan):
    frames, rows, width, chans = values.shape
    wide[...] = jnp.zeros_like(wide)
    wide[:, 1 : rows + 1, 8 : 8 + width, :] = values[...]
    for (dh, dw), (start, size) in plan.items():
        row = rows + 1 if dh < 0 else 0
        col = 8 + width if dw < 0 else 7
        for f in range(frames):
            if dw == 0:
                wide[f, row, 8 : 8 + width, :] = border[pl.ds(start + f * width, width), :]
            elif dh == 0:
                for r in range(rows):
                    wide[f, r + 1, pl.ds(col, 1), :] = border[pl.ds(start + f * rows + r, 1), :]
            else:
                wide[f, row, pl.ds(col, 1), :] = border[pl.ds(start + f, 1), :]


def fill_patches(patches, shifted, wide, width, lead, tail):
    frames, rows_wide, _, chans = wide.shape
    rows = rows_wide - 2
    for e in range(3):
        shifted[e, lead[0] : lead[0] + frames] = wide[:, :, 7 + e : 7 + e + width, :].astype(jnp.bfloat16)
        for f in range(lead[0]):
            if lead[1]:
                shifted[e, f] = wide[0, :, 7 + e : 7 + e + width, :].astype(jnp.bfloat16)
            else:
                shifted[e, f] = jnp.zeros((rows_wide, width, chans), jnp.bfloat16)
        for f in range(tail):
            shifted[e, lead[0] + frames + f] = jnp.zeros((rows_wide, width, chans), jnp.bfloat16)
    count = lead[0] + frames + tail - 2
    for tap in range(27):
        t, b, e = tap // 9, tap // 3 % 3, tap % 3
        piece = shifted[e, t : t + count, b : b + rows]
        patches[:, tap * chans : (tap + 1) * chans] = piece.reshape(count * rows * width, chans)


def total_mean(x, count):
    return jnp.sum(x, axis=1, keepdims=True) / count


def forward_kernel(values, border, all_stat, mask, kernel, gain, shift, *rest, plan, count, add, conv):
    rest = list(rest)
    base = rest.pop(0) if add else None
    normed, scale_out, patches = rest[:3]
    rest = rest[3:]
    if conv:
        result, stat, edges = rest[:3]
        rest = rest[3:]
    wide, shifted = rest
    frames, rows, width, chans = values.shape
    local = rows * width
    unpack(wide, values, border, plan)
    all_sums, all_squares = all_stat[:, :frames], all_stat[:, frames:]
    mean = total_mean(jnp.sum(all_sums, axis=0), count)
    gap = all_sums * (1.0 / local) - mean[None]
    var = total_mean(jnp.sum(all_squares + local * gap * gap, axis=0), count)
    inv_std = lax.rsqrt(var + norm_eps)
    scale_out[...] = jnp.broadcast_to(inv_std, (frames, chans))
    for f in range(frames):
        x = (wide[f] - mean[f : f + 1][None]) * inv_std[f : f + 1][None]
        normed[f] = x
        pre = x * gain[...][None] + shift[...][None]
        wide[f] = pre * jax.nn.sigmoid(pre) * mask[...]
    fill_patches(patches, shifted, wide, width, (2, True), 0)
    if not conv:
        return
    out = jnp.dot(patches[...], kernel[...], preferred_element_type=jnp.float32).reshape(frames, rows, width, chans)
    if add:
        out = out + base[...]
    result[...] = out
    fill_stat(stat, out)
    pack(edges, result, plan)


def fill_stat(stat, out):
    frames, rows, width, _ = out.shape
    sums = jnp.sum(out, axis=(1, 2))
    stat[:frames] = sums
    centred = out - (sums * (1.0 / (rows * width)))[:, None, None]
    stat[frames:] = jnp.sum(centred * centred, axis=(1, 2))


def start_kernel(inputs, upstream, values, up, stat, edges, up_edges, *, plan):
    values[...] = inputs[...].astype(jnp.float32)
    up[...] = upstream[...].astype(jnp.float32)
    fill_stat(stat, values[...])
    pack(edges, values, plan)
    pack(up_edges, up, plan)


def backward_kernel(*refs, plan, count, normed_in, add):
    refs = list(refs)
    values, border, all_stat, mask, kernel, gain, shift, normed, patches = refs[:9]
    refs = refs[9:]
    if normed_in:
        last_normed, last_inv, last_gain = refs[:3]
        refs = refs[3:]
    base = refs.pop(0) if add else None
    keep, term, dn_out, stat, edges, wide, shifted, out_patches = refs
    frames, rows, width, chans = values.shape
    unpack(wide, values, border, plan)
    if normed_in:
        total = jnp.sum(all_stat[...], axis=0)
        s1 = total_mean(total[:frames] * last_gain[...], count)
        s2 = total_mean(total[frames:] * last_gain[...], count)
        for f in range(frames):
            into = last_inv[f : f + 1][None] * (
                wide[f] * last_gain[...][None] - s1[f : f + 1][None] - last_normed[f] * s2[f : f + 1][None]
            )
            into = into * mask[...]
            if add:
                into = into + base[f]
            wide[f] = into
    keep[...] = wide[...]
    flat = wide[:, 1 : rows + 1, 8 : 8 + width, :].astype(jnp.bfloat16).reshape(frames * rows * width, chans)
    term[...] = lax.dot_general(patches[...], flat, (((0,), (0,)), ((), ())), preferred_element_type=jnp.float32)
    fill_patches(out_patches, shifted, wide, width, (2, False), 2)
    back = jnp.zeros(((frames + 2) * rows * width, chans), jnp.float32)
    for tap in range(27):
        back = back + lax.dot_general(
            out_patches[:, tap * chans : (tap + 1) * chans],
            kernel[(26 - tap) * chans : (27 - tap) * chans, :],
            (((1,), (1,)), ((), ())),
            preferred_element_type=jnp.float32,
        )
    back = back.reshape(frames + 2, rows, width, chans)
    for f in range(frames):
        grad = back[0] + back[1] + back[2] if f == 0 else back[f + 2]
        x = normed[f, 1 : rows + 1, 8 : 8 + width, :]
        pre = x * gain[...][None] + shift[...][None]
        sig = jax.nn.sigmoid(pre)
        dn = grad * (sig * (1.0 + pre * (1.0 - sig)))
        dn_out[f] = dn
        stat[f : f + 1] = jnp.sum(dn, axis=(0, 1))[None]
        stat[frames + f : frames + f + 1] = jnp.sum(dn * x, axis=(0, 1))[None]
    pack(edges, dn_out, plan)


def call(body, args, outs, scratch):
    vmem = pl.BlockSpec(memory_space=pltpu.VMEM)
    return pl.pallas_call(
        body,
        out_shape=tuple(jax.ShapeDtypeStruct(shape, dtype) for shape, dtype in outs),
        in_specs=[vmem] * len(args),
        out_specs=(vmem,) * len(outs),
        scratch_shapes=[pltpu.VMEM(shape, dtype) for shape, dtype in scratch],
        compiler_params=pltpu.CompilerParams(vmem_limit_bytes=40 * 2**20),
    )(*args)


def body(inputs, upstream, kernels, norm_gain, norm_shift):
    frames, rows, width, chans = inputs.shape
    rows_n, cols_n = lax.axis_size("ha"), lax.axis_size("wa")
    total_rows, total_width = rows * rows_n, width * cols_n
    count = total_rows * total_width * chans
    scale = 1.0 / math.sqrt(frames * total_rows * total_width)
    layers = kernels.shape[0]
    a, w = lax.axis_index("ha"), lax.axis_index("wa")
    row_id = a * rows - 1 + jnp.arange(rows + 2)
    col_id = w * width - 8 + jnp.arange(width + 16)
    inside = ((row_id >= 0) & (row_id < total_rows))[:, None] & ((col_id >= 0) & (col_id < total_width))[None]
    mask = jnp.broadcast_to(inside[:, :, None].astype(jnp.float32), (rows + 2, width + 16, chans))
    plan, edge_rows = border_plan(frames, rows, width)
    f32, bf16 = jnp.float32, jnp.bfloat16
    own = ((frames, rows, width, chans), f32)
    stat_t = ((2 * frames, chans), f32)
    edge_t = ((edge_rows, chans), f32)
    wide_t = ((frames, rows + 2, width + 16, chans), f32)
    inv_t = ((frames, chans), f32)
    patch_t = ((frames * rows * width, 27 * chans), bf16)
    gains = [norm_gain[j : j + 1] for j in range(layers)]
    shifts = [norm_shift[j : j + 1] for j in range(layers)]

    values, up, stat, edges, up_edges = call(
        lambda *r: start_kernel(*r, plan=plan), [inputs, upstream], [own, own, stat_t, edge_t, edge_t], []
    )
    stream = values
    saved = []
    for layer in range(layers):
        all_stat, border = exchange(stat, edges, plan, rows_n, cols_n)
        add = layer % 2 == 1 and layer < layers - 1
        conv = layer < layers - 1
        args = [values, border, all_stat, mask, kernels[layer], gains[layer], shifts[layer]]
        if add:
            args.append(stream)
        outs = [wide_t, inv_t, patch_t] + ([own, stat_t, edge_t] if conv else [])

        def run(*r, add=add, conv=conv):
            forward_kernel(*r, plan=plan, count=count, add=add, conv=conv)

        got = call(run, args, outs, [wide_t, ((3, frames + 2, rows + 2, width, chans), bf16)])
        saved.append(got[:3])
        if conv:
            values, stat, edges = got[3:]
            if add:
                stream = values

    terms, gain_sums, shift_sums = [None] * layers, [None] * layers, [None] * layers
    values, edges, stat = up, up_edges, jnp.zeros(stat_t[0], f32)
    grad_stream = None
    for layer in range(layers - 1, -1, -1):
        all_stat, border = exchange(stat, edges, plan, rows_n, cols_n)
        args = [values, border, all_stat, mask, kernels[layer], gains[layer], shifts[layer], saved[layer][0], saved[layer][2]]
        normed_in = layer < layers - 1
        add = normed_in and layer % 2 == 1
        if normed_in:
            args += [saved[layer + 1][0], saved[layer + 1][1], gains[layer + 1]]
            total = jnp.sum(all_stat, axis=0)
            shift_sums[layer + 1] = jnp.sum(total[:frames], axis=0)
            gain_sums[layer + 1] = jnp.sum(total[frames:], axis=0)
        if add:
            args.append(grad_stream)

        def run_back(*r, normed_in=normed_in, add=add):
            backward_kernel(*r, plan=plan, count=count, normed_in=normed_in, add=add)

        keep, term, values, stat, edges = call(
            run_back,
            args,
            [wide_t, ((27 * chans, chans), f32), own, stat_t, edge_t],
            [
                wide_t,
                ((3, frames + 4, rows + 2, width, chans), bf16),
                (((frames + 2) * rows * width, 27 * chans), bf16),
            ],
        )
        if layer % 2 == 1:
            grad_stream = keep
        share = lax.psum_scatter(term.reshape(27, chans, chans), ("ha", "wa"), scatter_dimension=1, tiled=True)
        terms[layer] = share.reshape(27, -1)
    all_stat, _ = exchange(stat, edges, plan, rows_n, cols_n)
    total = jnp.sum(all_stat, axis=0)
    shift_sums[0] = jnp.sum(total[:frames], axis=0)
    gain_sums[0] = jnp.sum(total[frames:], axis=0)
    s1 = (jnp.sum(total[:frames] * norm_gain[0], axis=1) / count)[:, None, None, None]
    s2 = (jnp.sum(total[frames:] * norm_gain[0], axis=1) / count)[:, None, None, None]
    cut = (slice(None), slice(1, rows + 1), slice(8, 8 + width))
    into = saved[0][1][:, None, None] * (values * norm_gain[0] - s1 - saved[0][0][cut] * s2)
    input_grad = (grad_stream[cut] + into).astype(jnp.bfloat16)
    norm_grads = jnp.stack([jnp.stack(gain_sums), jnp.stack(shift_sums)]) * scale
    return (input_grad, jnp.stack(terms) * scale, norm_grads)


def solution(mesh):
    return jax.shard_map(
        body,
        mesh=mesh,
        in_specs=(P("grp", "ha", "wa", None), P("grp", "ha", "wa", None), P(), P(), P()),
        out_specs=(P("grp", "ha", "wa", None), P("grp", None, ("ha", "wa")), P("grp", None, None)),
        check_vma=False,
    )
```

```python
import math

import jax
import jax.numpy as jnp
from jax import lax
from jax.experimental import pallas as pl
from jax.experimental.pallas import tpu as pltpu
from jax.sharding import PartitionSpec as P

norm_eps = 1e-06
MESH = pl.DeviceIdType.MESH


def exchange_kernel(stat, edges, all_stat, border, stat_send, stat_recv, edge_send, edge_recv, *, rows_n, cols_n, pieces):
    n = rows_n * cols_n
    g, a, w = lax.axis_index("grp"), lax.axis_index("ha"), lax.axis_index("wa")
    me = a * cols_n + w
    border[...] = jnp.zeros_like(border)
    barrier = pltpu.get_barrier_semaphore()

    def device(index):
        return (g, lax.div(index, cols_n), lax.rem(index, cols_n))

    for k in range(1, n):
        pl.semaphore_signal(barrier, inc=1, device_id=device(lax.rem(me + k, n)), device_id_type=MESH)
    pl.semaphore_wait(barrier, n - 1)
    plans = []
    for i, (dh, dw, src, dst, size) in enumerate(pieces):
        ok_to = (a + dh >= 0) & (a + dh < rows_n) & (w + dw >= 0) & (w + dw < cols_n)
        ok_from = (a - dh >= 0) & (a - dh < rows_n) & (w - dw >= 0) & (w - dw < cols_n)
        copy = pltpu.make_async_remote_copy(
            edges.at[pl.ds(src, size)],
            border.at[pl.ds(dst, size)],
            edge_send.at[i],
            edge_recv.at[i],
            device_id=(g, a + dh, w + dw),
            device_id_type=MESH,
        )
        plans.append((ok_to, ok_from, copy))

        @pl.when(ok_to)
        def _():
            copy.start()

    all_stat[0] = stat[...]
    copies = []
    for k in range(1, n):
        copy = pltpu.make_async_remote_copy(
            stat,
            all_stat.at[k],
            stat_send.at[k],
            stat_recv.at[k],
            device_id=device(lax.rem(me + k, n)),
            device_id_type=MESH,
        )
        copy.start()
        copies.append(copy)
    for copy in copies:
        copy.wait()
    for ok_to, ok_from, copy in plans:

        @pl.when(ok_to)
        def _():
            copy.wait_send()

        @pl.when(ok_from)
        def _():
            copy.wait_recv()


def border_plan(frames, rows, width):
    moves = [(-1, 0, frames * width), (1, 0, frames * width), (0, -1, frames * rows), (0, 1, frames * rows)]
    moves += [(dh, dw, 8 * pl.cdiv(frames, 8)) for dh in (-1, 1) for dw in (-1, 1)]
    plan, offset = {}, 0
    for dh, dw, size in moves:
        plan[dh, dw] = (offset, size)
        offset += size
    return plan, offset


def exchange(stat, packed, plan, rows_n, cols_n):
    pieces = [(dh, dw, start, start, size) for (dh, dw), (start, size) in plan.items()]
    n = rows_n * cols_n
    vmem = pl.BlockSpec(memory_space=pltpu.VMEM)

    def run(*args):
        return exchange_kernel(*args, rows_n=rows_n, cols_n=cols_n, pieces=pieces)

    return pl.pallas_call(
        run,
        out_shape=(
            jax.ShapeDtypeStruct((n,) + stat.shape, jnp.float32),
            jax.ShapeDtypeStruct(packed.shape, jnp.float32),
        ),
        in_specs=[vmem, vmem],
        out_specs=(vmem, vmem),
        scratch_shapes=[
            pltpu.SemaphoreType.DMA((n,)),
            pltpu.SemaphoreType.DMA((n,)),
            pltpu.SemaphoreType.DMA((8,)),
            pltpu.SemaphoreType.DMA((8,)),
        ],
        compiler_params=pltpu.CompilerParams(collective_id=0, has_side_effects=True),
    )(stat, packed)


def pack(edges, values, plan):
    frames, rows, width, chans = values.shape
    for (dh, dw), (start, size) in plan.items():
        row = 0 if dh < 0 else rows - 1
        col = 0 if dw < 0 else width - 1
        for f in range(frames):
            if dw == 0:
                edges[pl.ds(start + f * width, width), :] = values[f, row]
            elif dh == 0:
                for r in range(rows):
                    edges[pl.ds(start + f * rows + r, 1), :] = values[f, r, pl.ds(col, 1), :]
            else:
                edges[pl.ds(start + f, 1), :] = values[f, row, pl.ds(col, 1), :]
        if dh != 0 and dw != 0 and size > frames:
            edges[pl.ds(start + frames, size - frames), :] = jnp.zeros((size - frames, chans), jnp.float32)


def unpack(wide, values, border, plan):
    frames, rows, width, chans = values.shape
    wide[...] = jnp.zeros_like(wide)
    wide[:, 1 : rows + 1, 8 : 8 + width, :] = values[...]
    for (dh, dw), (start, size) in plan.items():
        row = rows + 1 if dh < 0 else 0
        col = 8 + width if dw < 0 else 7
        for f in range(frames):
            if dw == 0:
                wide[f, row, 8 : 8 + width, :] = border[pl.ds(start + f * width, width), :]
            elif dh == 0:
                for r in range(rows):
                    wide[f, r + 1, pl.ds(col, 1), :] = border[pl.ds(start + f * rows + r, 1), :]
            else:
                wide[f, row, pl.ds(col, 1), :] = border[pl.ds(start + f, 1), :]


def fill_patches(patches, shifted, wide, width, lead, tail):
    frames, rows_wide, _, chans = wide.shape
    rows = rows_wide - 2
    for e in range(3):
        shifted[e, lead[0] : lead[0] + frames] = wide[:, :, 7 + e : 7 + e + width, :].astype(jnp.bfloat16)
        for f in range(lead[0]):
            if lead[1]:
                shifted[e, f] = wide[0, :, 7 + e : 7 + e + width, :].astype(jnp.bfloat16)
            else:
                shifted[e, f] = jnp.zeros((rows_wide, width, chans), jnp.bfloat16)
        for f in range(tail):
            shifted[e, lead[0] + frames + f] = jnp.zeros((rows_wide, width, chans), jnp.bfloat16)
    count = lead[0] + frames + tail - 2
    for tap in range(27):
        t, b, e = tap // 9, tap // 3 % 3, tap % 3
        piece = shifted[e, t : t + count, b : b + rows]
        patches[:, tap * chans : (tap + 1) * chans] = piece.reshape(count * rows * width, chans)


def total_mean(x, count):
    return jnp.sum(x, axis=1, keepdims=True) / count


def forward_kernel(values, border, all_stat, mask, kernel, gain, shift, *rest, plan, count, add, conv):
    rest = list(rest)
    base = rest.pop(0) if add else None
    normed, scale_out, patches = rest[:3]
    rest = rest[3:]
    if conv:
        result, stat, edges = rest[:3]
        rest = rest[3:]
    wide, shifted = rest
    frames, rows, width, chans = values.shape
    local = rows * width
    unpack(wide, values, border, plan)
    all_sums, all_squares = all_stat[:, :frames], all_stat[:, frames:]
    mean = total_mean(jnp.sum(all_sums, axis=0), count)
    gap = all_sums * (1.0 / local) - mean[None]
    var = total_mean(jnp.sum(all_squares + local * gap * gap, axis=0), count)
    inv_std = lax.rsqrt(var + norm_eps)
    scale_out[...] = jnp.broadcast_to(inv_std, (frames, chans))
    for f in range(frames):
        x = (wide[f] - mean[f : f + 1][None]) * inv_std[f : f + 1][None]
        normed[f] = x
        pre = x * gain[...][None] + shift[...][None]
        wide[f] = pre * jax.nn.sigmoid(pre) * mask[...]
    fill_patches(patches, shifted, wide, width, (2, True), 0)
    if not conv:
        return
    out = jnp.dot(patches[...], kernel[...], preferred_element_type=jnp.float32).reshape(frames, rows, width, chans)
    if add:
        out = out + base[...]
    result[...] = out
    fill_stat(stat, out)
    pack(edges, result, plan)


def fill_stat(stat, out):
    frames, rows, width, _ = out.shape
    sums = jnp.sum(out, axis=(1, 2))
    stat[:frames] = sums
    centred = out - (sums * (1.0 / (rows * width)))[:, None, None]
    stat[frames:] = jnp.sum(centred * centred, axis=(1, 2))


def start_kernel(inputs, upstream, values, up, stat, edges, up_edges, *, plan):
    values[...] = inputs[...].astype(jnp.float32)
    up[...] = upstream[...].astype(jnp.float32)
    fill_stat(stat, values[...])
    pack(edges, values, plan)
    pack(up_edges, up, plan)


def backward_kernel(*refs, plan, count, normed_in, add):
    refs = list(refs)
    values, border, all_stat, mask, kernel, gain, shift, normed, patches = refs[:9]
    refs = refs[9:]
    if normed_in:
        last_normed, last_inv, last_gain = refs[:3]
        refs = refs[3:]
    base = refs.pop(0) if add else None
    keep, term, dn_out, stat, edges, wide, shifted, out_patches = refs
    frames, rows, width, chans = values.shape
    unpack(wide, values, border, plan)
    if normed_in:
        total = jnp.sum(all_stat[...], axis=0)
        s1 = total_mean(total[:frames] * last_gain[...], count)
        s2 = total_mean(total[frames:] * last_gain[...], count)
        for f in range(frames):
            into = last_inv[f : f + 1][None] * (
                wide[f] * last_gain[...][None] - s1[f : f + 1][None] - last_normed[f] * s2[f : f + 1][None]
            )
            into = into * mask[...]
            if add:
                into = into + base[f]
            wide[f] = into
    keep[...] = wide[...]
    flat = wide[:, 1 : rows + 1, 8 : 8 + width, :].astype(jnp.bfloat16).reshape(frames * rows * width, chans)
    term[...] = lax.dot_general(patches[...], flat, (((0,), (0,)), ((), ())), preferred_element_type=jnp.float32)
    fill_patches(out_patches, shifted, wide, width, (2, False), 2)
    back = jnp.zeros(((frames + 2) * rows * width, chans), jnp.float32)
    for tap in range(27):
        back = back + lax.dot_general(
            out_patches[:, tap * chans : (tap + 1) * chans],
            kernel[(26 - tap) * chans : (27 - tap) * chans, :],
            (((1,), (1,)), ((), ())),
            preferred_element_type=jnp.float32,
        )
    back = back.reshape(frames + 2, rows, width, chans)
    for f in range(frames):
        grad = back[0] + back[1] + back[2] if f == 0 else back[f + 2]
        x = normed[f, 1 : rows + 1, 8 : 8 + width, :]
        pre = x * gain[...][None] + shift[...][None]
        sig = jax.nn.sigmoid(pre)
        dn = grad * (sig * (1.0 + pre * (1.0 - sig)))
        dn_out[f] = dn
        stat[f : f + 1] = jnp.sum(dn, axis=(0, 1))[None]
        stat[frames + f : frames + f + 1] = jnp.sum(dn * x, axis=(0, 1))[None]
    pack(edges, dn_out, plan)


def call(body, args, outs, scratch):
    vmem = pl.BlockSpec(memory_space=pltpu.VMEM)
    return pl.pallas_call(
        body,
        out_shape=tuple(jax.ShapeDtypeStruct(shape, dtype) for shape, dtype in outs),
        in_specs=[vmem] * len(args),
        out_specs=(vmem,) * len(outs),
        scratch_shapes=[pltpu.VMEM(shape, dtype) for shape, dtype in scratch],
        compiler_params=pltpu.CompilerParams(vmem_limit_bytes=40 * 2**20),
    )(*args)


def scatter_kernel(*refs, layers, rows_n, scale):
    terms, refs = refs[:layers], refs[layers:]
    result, got0, sum0, got1, sum1, got2, send0, recv0, send1, recv1, send2, recv2 = refs
    g, a, w = lax.axis_index("grp"), lax.axis_index("ha"), lax.axis_index("wa")
    low, high = lax.rem(w, 2), lax.div(w, 2)
    near = (g, a, w + 1 - 2 * low)
    far = (g, a, w + 2 - 4 * high)
    rows_to = [lax.rem(a + k, rows_n) for k in range(rows_n)]
    barrier = pltpu.get_barrier_semaphore()
    for device in [near, far] + [(g, rows_to[k], w) for k in range(1, rows_n)]:
        pl.semaphore_signal(barrier, inc=1, device_id=device, device_id_type=MESH)
    pl.semaphore_wait(barrier, rows_n + 1)

    def send(src, dst, send_sem, recv_sem, device):
        copy = pltpu.make_async_remote_copy(src, dst, send_sem, recv_sem, device_id=device, device_id_type=MESH)
        copy.start()
        return copy

    first = [
        send(terms[j].at[1 - low], got0.at[j], send0.at[j], recv0.at[j], near) for j in range(layers)
    ]
    second, third = [], []
    for j in range(layers):
        first[j].wait()
        for b in range(2):
            total = terms[j][low, b].astype(jnp.float32) + got0[j, b].astype(jnp.float32)
            sum0[j, b] = total.astype(jnp.bfloat16)
        second.append(send(sum0.at[j, 1 - high], got1.at[j], send1.at[j], recv1.at[j], far))
    for j in range(layers):
        second[j].wait()
        total = sum0[j, high].astype(jnp.float32) + got1[j].astype(jnp.float32)
        sum1[j] = total.astype(jnp.bfloat16)
        third.append(
            [
                send(sum1.at[j, rows_to[k]], got2.at[j, k], send2.at[j, k], recv2.at[j, k], (g, rows_to[k], w))
                for k in range(1, rows_n)
            ]
        )
    for j in range(layers):
        total = sum1[j, a].astype(jnp.float32)
        for k in range(1, rows_n):
            third[j][k - 1].wait()
            total = total + got2[j, k].astype(jnp.float32)
        result[j] = total * scale


def scatter_terms(terms, chans, rows_n, cols_n, scale):
    layers = len(terms)
    share = chans // (rows_n * cols_n)
    size = 16 * pl.cdiv(27 * share, 16)
    shape = (2, 2, rows_n, size, chans)
    vmem = pl.BlockSpec(memory_space=pltpu.VMEM)
    dma = pltpu.SemaphoreType.DMA

    def run(*refs):
        scatter_kernel(*refs, layers=layers, rows_n=rows_n, scale=scale)

    out = pl.pallas_call(
        run,
        out_shape=jax.ShapeDtypeStruct((layers, size, chans), jnp.float32),
        in_specs=[vmem] * layers,
        out_specs=vmem,
        scratch_shapes=[
            pltpu.VMEM((layers,) + shape[1:], jnp.bfloat16),
            pltpu.VMEM((layers,) + shape[1:], jnp.bfloat16),
            pltpu.VMEM((layers,) + shape[2:], jnp.bfloat16),
            pltpu.VMEM((layers,) + shape[2:], jnp.bfloat16),
            pltpu.VMEM((layers,) + shape[2:], jnp.bfloat16),
            dma((layers,)),
            dma((layers,)),
            dma((layers,)),
            dma((layers,)),
            dma((layers, rows_n)),
            dma((layers, rows_n)),
        ],
        compiler_params=pltpu.CompilerParams(collective_id=1, has_side_effects=True, vmem_limit_bytes=40 * 2**20),
    )(*terms)
    return out[:, : 27 * share].reshape(layers, 27, share * chans)


def spread_shares(term, chans, rows_n, cols_n):
    share = chans // (rows_n * cols_n)
    parts = term.reshape(27, rows_n, 2, 2, share, chans).transpose(3, 2, 1, 0, 4, 5)
    parts = parts.reshape(2, 2, rows_n, 27 * share, chans).astype(jnp.bfloat16)
    return jnp.pad(parts, ((0, 0), (0, 0), (0, 0), (0, -27 * share % 16), (0, 0)))


def body(inputs, upstream, kernels, norm_gain, norm_shift):
    frames, rows, width, chans = inputs.shape
    rows_n, cols_n = lax.axis_size("ha"), lax.axis_size("wa")
    total_rows, total_width = rows * rows_n, width * cols_n
    count = total_rows * total_width * chans
    scale = 1.0 / math.sqrt(frames * total_rows * total_width)
    layers = kernels.shape[0]
    a, w = lax.axis_index("ha"), lax.axis_index("wa")
    row_id = a * rows - 1 + jnp.arange(rows + 2)
    col_id = w * width - 8 + jnp.arange(width + 16)
    inside = ((row_id >= 0) & (row_id < total_rows))[:, None] & ((col_id >= 0) & (col_id < total_width))[None]
    mask = jnp.broadcast_to(inside[:, :, None].astype(jnp.float32), (rows + 2, width + 16, chans))
    plan, edge_rows = border_plan(frames, rows, width)
    f32, bf16 = jnp.float32, jnp.bfloat16
    own = ((frames, rows, width, chans), f32)
    stat_t = ((2 * frames, chans), f32)
    edge_t = ((edge_rows, chans), f32)
    wide_t = ((frames, rows + 2, width + 16, chans), f32)
    inv_t = ((frames, chans), f32)
    patch_t = ((frames * rows * width, 27 * chans), bf16)
    gains = [norm_gain[j : j + 1] for j in range(layers)]
    shifts = [norm_shift[j : j + 1] for j in range(layers)]

    values, up, stat, edges, up_edges = call(
        lambda *r: start_kernel(*r, plan=plan), [inputs, upstream], [own, own, stat_t, edge_t, edge_t], []
    )
    stream = values
    saved = []
    for layer in range(layers):
        all_stat, border = exchange(stat, edges, plan, rows_n, cols_n)
        add = layer % 2 == 1 and layer < layers - 1
        conv = layer < layers - 1
        args = [values, border, all_stat, mask, kernels[layer], gains[layer], shifts[layer]]
        if add:
            args.append(stream)
        outs = [wide_t, inv_t, patch_t] + ([own, stat_t, edge_t] if conv else [])

        def run(*r, add=add, conv=conv):
            forward_kernel(*r, plan=plan, count=count, add=add, conv=conv)

        got = call(run, args, outs, [wide_t, ((3, frames + 2, rows + 2, width, chans), bf16)])
        saved.append(got[:3])
        if conv:
            values, stat, edges = got[3:]
            if add:
                stream = values

    terms, gain_sums, shift_sums = [None] * layers, [None] * layers, [None] * layers
    values, edges, stat = up, up_edges, jnp.zeros(stat_t[0], f32)
    grad_stream = None
    for layer in range(layers - 1, -1, -1):
        all_stat, border = exchange(stat, edges, plan, rows_n, cols_n)
        args = [values, border, all_stat, mask, kernels[layer], gains[layer], shifts[layer], saved[layer][0], saved[layer][2]]
        normed_in = layer < layers - 1
        add = normed_in and layer % 2 == 1
        if normed_in:
            args += [saved[layer + 1][0], saved[layer + 1][1], gains[layer + 1]]
            total = jnp.sum(all_stat, axis=0)
            shift_sums[layer + 1] = jnp.sum(total[:frames], axis=0)
            gain_sums[layer + 1] = jnp.sum(total[frames:], axis=0)
        if add:
            args.append(grad_stream)

        def run_back(*r, normed_in=normed_in, add=add):
            backward_kernel(*r, plan=plan, count=count, normed_in=normed_in, add=add)

        keep, term, values, stat, edges = call(
            run_back,
            args,
            [wide_t, ((27 * chans, chans), f32), own, stat_t, edge_t],
            [
                wide_t,
                ((3, frames + 4, rows + 2, width, chans), bf16),
                (((frames + 2) * rows * width, 27 * chans), bf16),
            ],
        )
        if layer % 2 == 1:
            grad_stream = keep
        terms[layer] = spread_shares(term, chans, rows_n, cols_n)
    all_stat, _ = exchange(stat, edges, plan, rows_n, cols_n)
    total = jnp.sum(all_stat, axis=0)
    shift_sums[0] = jnp.sum(total[:frames], axis=0)
    gain_sums[0] = jnp.sum(total[frames:], axis=0)
    s1 = (jnp.sum(total[:frames] * norm_gain[0], axis=1) / count)[:, None, None, None]
    s2 = (jnp.sum(total[frames:] * norm_gain[0], axis=1) / count)[:, None, None, None]
    cut = (slice(None), slice(1, rows + 1), slice(8, 8 + width))
    into = saved[0][1][:, None, None] * (values * norm_gain[0] - s1 - saved[0][0][cut] * s2)
    input_grad = (grad_stream[cut] + into).astype(jnp.bfloat16)
    norm_grads = jnp.stack([jnp.stack(gain_sums), jnp.stack(shift_sums)]) * scale
    kernel_grads = scatter_terms(terms, chans, rows_n, cols_n, scale)
    return (input_grad, kernel_grads, norm_grads)


def solution(mesh):
    return jax.shard_map(
        body,
        mesh=mesh,
        in_specs=(P("grp", "ha", "wa", None), P("grp", "ha", "wa", None), P(), P(), P()),
        out_specs=(P("grp", "ha", "wa", None), P("grp", None, ("ha", "wa")), P("grp", None, None)),
        check_vma=False,
    )
```

```python
import math

import jax
import jax.numpy as jnp
from jax import lax
from jax.experimental import pallas as pl
from jax.experimental.pallas import tpu as pltpu
from jax.sharding import PartitionSpec as P

norm_eps = 1e-06
MESH = pl.DeviceIdType.MESH


def exchange_kernel(stat, edges, all_stat, border, stat_send, stat_recv, edge_send, edge_recv, *, rows_n, cols_n, pieces):
    n = rows_n * cols_n
    g, a, w = lax.axis_index("grp"), lax.axis_index("ha"), lax.axis_index("wa")
    me = a * cols_n + w
    border[...] = jnp.zeros_like(border)
    barrier = pltpu.get_barrier_semaphore()

    def device(index):
        return (g, lax.div(index, cols_n), lax.rem(index, cols_n))

    for k in range(1, n):
        pl.semaphore_signal(barrier, inc=1, device_id=device(lax.rem(me + k, n)), device_id_type=MESH)
    pl.semaphore_wait(barrier, n - 1)
    plans = []
    for i, (dh, dw, src, dst, size) in enumerate(pieces):
        ok_to = (a + dh >= 0) & (a + dh < rows_n) & (w + dw >= 0) & (w + dw < cols_n)
        ok_from = (a - dh >= 0) & (a - dh < rows_n) & (w - dw >= 0) & (w - dw < cols_n)
        copy = pltpu.make_async_remote_copy(
            edges.at[pl.ds(src, size)],
            border.at[pl.ds(dst, size)],
            edge_send.at[i],
            edge_recv.at[i],
            device_id=(g, a + dh, w + dw),
            device_id_type=MESH,
        )
        plans.append((ok_to, ok_from, copy))

        @pl.when(ok_to)
        def _():
            copy.start()

    all_stat[0] = stat[...]
    copies = []
    for k in range(1, n):
        copy = pltpu.make_async_remote_copy(
            stat,
            all_stat.at[k],
            stat_send.at[k],
            stat_recv.at[k],
            device_id=device(lax.rem(me + k, n)),
            device_id_type=MESH,
        )
        copy.start()
        copies.append(copy)
    for copy in copies:
        copy.wait()
    for ok_to, ok_from, copy in plans:

        @pl.when(ok_to)
        def _():
            copy.wait_send()

        @pl.when(ok_from)
        def _():
            copy.wait_recv()


def border_plan(frames, rows, width):
    moves = [(-1, 0, frames * width), (1, 0, frames * width), (0, -1, frames * rows), (0, 1, frames * rows)]
    moves += [(dh, dw, 8 * pl.cdiv(frames, 8)) for dh in (-1, 1) for dw in (-1, 1)]
    plan, offset = {}, 0
    for dh, dw, size in moves:
        plan[dh, dw] = (offset, size)
        offset += size
    return plan, offset


def exchange(stat, packed, plans, rows_n, cols_n, collective_id):
    pieces = [(dh, dw, start, start, size) for plan in plans for (dh, dw), (start, size) in plan.items()]
    n = rows_n * cols_n
    vmem = pl.BlockSpec(memory_space=pltpu.VMEM)

    def run(*args):
        return exchange_kernel(*args, rows_n=rows_n, cols_n=cols_n, pieces=pieces)

    return pl.pallas_call(
        run,
        out_shape=(
            jax.ShapeDtypeStruct((n,) + stat.shape, jnp.float32),
            jax.ShapeDtypeStruct(packed.shape, jnp.float32),
        ),
        in_specs=[vmem, vmem],
        out_specs=(vmem, vmem),
        scratch_shapes=[
            pltpu.SemaphoreType.DMA((n,)),
            pltpu.SemaphoreType.DMA((n,)),
            pltpu.SemaphoreType.DMA((len(pieces),)),
            pltpu.SemaphoreType.DMA((len(pieces),)),
        ],
        compiler_params=pltpu.CompilerParams(collective_id=collective_id, has_side_effects=True),
    )(stat, packed)


def pack(edges, values, plan):
    frames, rows, width, chans = values.shape
    for (dh, dw), (start, size) in plan.items():
        row = 0 if dh < 0 else rows - 1
        col = 0 if dw < 0 else width - 1
        for f in range(frames):
            if dw == 0:
                edges[pl.ds(start + f * width, width), :] = values[f, row]
            elif dh == 0:
                for r in range(rows):
                    edges[pl.ds(start + f * rows + r, 1), :] = values[f, r, pl.ds(col, 1), :]
            else:
                edges[pl.ds(start + f, 1), :] = values[f, row, pl.ds(col, 1), :]
        if dh != 0 and dw != 0 and size > frames:
            edges[pl.ds(start + frames, size - frames), :] = jnp.zeros((size - frames, chans), jnp.float32)


def unpack(wide, values, border, plan):
    frames, rows, width, chans = values.shape
    wide[...] = jnp.zeros_like(wide)
    wide[:, 1 : rows + 1, 8 : 8 + width, :] = values[...]
    for (dh, dw), (start, size) in plan.items():
        row = rows + 1 if dh < 0 else 0
        col = 8 + width if dw < 0 else 7
        for f in range(frames):
            if dw == 0:
                wide[f, row, 8 : 8 + width, :] = border[pl.ds(start + f * width, width), :]
            elif dh == 0:
                for r in range(rows):
                    wide[f, r + 1, pl.ds(col, 1), :] = border[pl.ds(start + f * rows + r, 1), :]
            else:
                wide[f, row, pl.ds(col, 1), :] = border[pl.ds(start + f, 1), :]


def fill_patches(patches, shifted, wide, width, lead, tail):
    frames, rows_wide, _, chans = wide.shape
    rows = rows_wide - 2
    for e in range(3):
        shifted[e, lead[0] : lead[0] + frames] = wide[:, :, 7 + e : 7 + e + width, :].astype(jnp.bfloat16)
        for f in range(lead[0]):
            if lead[1]:
                shifted[e, f] = wide[0, :, 7 + e : 7 + e + width, :].astype(jnp.bfloat16)
            else:
                shifted[e, f] = jnp.zeros((rows_wide, width, chans), jnp.bfloat16)
        for f in range(tail):
            shifted[e, lead[0] + frames + f] = jnp.zeros((rows_wide, width, chans), jnp.bfloat16)
    count = lead[0] + frames + tail - 2
    for tap in range(27):
        t, b, e = tap // 9, tap // 3 % 3, tap % 3
        piece = shifted[e, t : t + count, b : b + rows]
        patches[:, tap * chans : (tap + 1) * chans] = piece.reshape(count * rows * width, chans)


def total_mean(x, count):
    return jnp.sum(x, axis=1, keepdims=True) / count


def forward_kernel(values, border, all_stat, mask, kernel, gain, shift, *rest, plan, count, add, conv):
    rest = list(rest)
    base = rest.pop(0) if add else None
    normed, scale_out, patches = rest[:3]
    rest = rest[3:]
    if conv:
        result, stat, edges = rest[:3]
        rest = rest[3:]
    wide, shifted = rest
    frames, rows, width, chans = values.shape
    local = rows * width
    unpack(wide, values, border, plan)
    all_sums, all_squares = all_stat[:, :frames], all_stat[:, frames:]
    mean = total_mean(jnp.sum(all_sums, axis=0), count)
    gap = all_sums * (1.0 / local) - mean[None]
    var = total_mean(jnp.sum(all_squares + local * gap * gap, axis=0), count)
    inv_std = lax.rsqrt(var + norm_eps)
    scale_out[...] = jnp.broadcast_to(inv_std, (frames, chans))
    for f in range(frames):
        x = (wide[f] - mean[f : f + 1][None]) * inv_std[f : f + 1][None]
        normed[f] = x
        pre = x * gain[...][None] + shift[...][None]
        wide[f] = pre * jax.nn.sigmoid(pre) * mask[...]
    fill_patches(patches, shifted, wide, width, (2, True), 0)
    if not conv:
        return
    out = jnp.dot(patches[...], kernel[...], preferred_element_type=jnp.float32).reshape(frames, rows, width, chans)
    if add:
        out = out + base[...]
    result[...] = out
    fill_stat(stat, out)
    pack(edges, result, plan)


def fill_stat(stat, out):
    frames, rows, width, _ = out.shape
    sums = jnp.sum(out, axis=(1, 2))
    stat[:frames] = sums
    centred = out - (sums * (1.0 / (rows * width)))[:, None, None]
    stat[frames:] = jnp.sum(centred * centred, axis=(1, 2))


def start_kernel(inputs, upstream, values, up, stat, edges, *, plan, up_plan):
    values[...] = inputs[...].astype(jnp.float32)
    up[...] = upstream[...].astype(jnp.float32)
    fill_stat(stat, values[...])
    pack(edges, values, plan)
    pack(edges, up, up_plan)


def backward_kernel(*refs, plan, from_plan, count, normed_in, add):
    refs = list(refs)
    values, border, all_stat, mask, kernel, gain, shift, normed, patches = refs[:9]
    refs = refs[9:]
    if normed_in:
        last_normed, last_inv, last_gain = refs[:3]
        refs = refs[3:]
    base = refs.pop(0) if add else None
    keep, term, dn_out, stat, edges, wide, shifted, out_patches = refs
    frames, rows, width, chans = values.shape
    unpack(wide, values, border, from_plan)
    if normed_in:
        total = jnp.sum(all_stat[...], axis=0)
        s1 = total_mean(total[:frames] * last_gain[...], count)
        s2 = total_mean(total[frames:] * last_gain[...], count)
        for f in range(frames):
            into = last_inv[f : f + 1][None] * (
                wide[f] * last_gain[...][None] - s1[f : f + 1][None] - last_normed[f] * s2[f : f + 1][None]
            )
            into = into * mask[...]
            if add:
                into = into + base[f]
            wide[f] = into
    keep[...] = wide[...]
    flat = wide[:, 1 : rows + 1, 8 : 8 + width, :].astype(jnp.bfloat16).reshape(frames * rows * width, chans)
    term[...] = lax.dot_general(patches[...], flat, (((0,), (0,)), ((), ())), preferred_element_type=jnp.float32)
    fill_patches(out_patches, shifted, wide, width, (2, False), 2)
    back = jnp.zeros(((frames + 2) * rows * width, chans), jnp.float32)
    for tap in range(27):
        back = back + lax.dot_general(
            out_patches[:, tap * chans : (tap + 1) * chans],
            kernel[(26 - tap) * chans : (27 - tap) * chans, :],
            (((1,), (1,)), ((), ())),
            preferred_element_type=jnp.float32,
        )
    back = back.reshape(frames + 2, rows, width, chans)
    for f in range(frames):
        grad = back[0] + back[1] + back[2] if f == 0 else back[f + 2]
        x = normed[f, 1 : rows + 1, 8 : 8 + width, :]
        pre = x * gain[...][None] + shift[...][None]
        sig = jax.nn.sigmoid(pre)
        dn = grad * (sig * (1.0 + pre * (1.0 - sig)))
        dn_out[f] = dn
        stat[f : f + 1] = jnp.sum(dn, axis=(0, 1))[None]
        stat[frames + f : frames + f + 1] = jnp.sum(dn * x, axis=(0, 1))[None]
    pack(edges, dn_out, plan)


def call(body, args, outs, scratch):
    vmem = pl.BlockSpec(memory_space=pltpu.VMEM)
    return pl.pallas_call(
        body,
        out_shape=tuple(jax.ShapeDtypeStruct(shape, dtype) for shape, dtype in outs),
        in_specs=[vmem] * len(args),
        out_specs=(vmem,) * len(outs),
        scratch_shapes=[pltpu.VMEM(shape, dtype) for shape, dtype in scratch],
        compiler_params=pltpu.CompilerParams(vmem_limit_bytes=58 * 2**20),
    )(*args)


def scatter_kernel(*refs, layers, rows_n, scale):
    terms, refs = refs[:layers], refs[layers:]
    result, got0, sum0, got1, sum1, got2, send0, recv0, send1, recv1, send2, recv2 = refs
    g, a, w = lax.axis_index("grp"), lax.axis_index("ha"), lax.axis_index("wa")
    low, high = lax.rem(w, 2), lax.div(w, 2)
    near = (g, a, w + 1 - 2 * low)
    far = (g, a, w + 2 - 4 * high)
    rows_to = [lax.rem(a + k, rows_n) for k in range(rows_n)]
    barrier = pltpu.get_barrier_semaphore()
    for device in [near, far] + [(g, rows_to[k], w) for k in range(1, rows_n)]:
        pl.semaphore_signal(barrier, inc=1, device_id=device, device_id_type=MESH)
    pl.semaphore_wait(barrier, rows_n + 1)

    def send(src, dst, send_sem, recv_sem, device):
        copy = pltpu.make_async_remote_copy(src, dst, send_sem, recv_sem, device_id=device, device_id_type=MESH)
        copy.start()
        return copy

    first = [
        send(terms[j].at[1 - low], got0.at[j], send0.at[j], recv0.at[j], near) for j in range(layers)
    ]
    second, third = [], []
    for j in range(layers):
        first[j].wait()
        for b in range(2):
            total = terms[j][low, b].astype(jnp.float32) + got0[j, b].astype(jnp.float32)
            sum0[j, b] = total.astype(jnp.bfloat16)
        second.append(send(sum0.at[j, 1 - high], got1.at[j], send1.at[j], recv1.at[j], far))
    for j in range(layers):
        second[j].wait()
        total = sum0[j, high].astype(jnp.float32) + got1[j].astype(jnp.float32)
        sum1[j] = total.astype(jnp.bfloat16)
        third.append(
            [
                send(sum1.at[j, rows_to[k]], got2.at[j, k], send2.at[j, k], recv2.at[j, k], (g, rows_to[k], w))
                for k in range(1, rows_n)
            ]
        )
    for j in range(layers):
        total = sum1[j, a].astype(jnp.float32)
        for k in range(1, rows_n):
            third[j][k - 1].wait()
            total = total + got2[j, k].astype(jnp.float32)
        result[j] = total * scale


def scatter_terms(terms, chans, rows_n, cols_n, scale):
    layers = len(terms)
    share = chans // (rows_n * cols_n)
    size = 16 * pl.cdiv(27 * share, 16)
    shape = (2, 2, rows_n, size, chans)
    vmem = pl.BlockSpec(memory_space=pltpu.VMEM)
    dma = pltpu.SemaphoreType.DMA

    def run(*refs):
        scatter_kernel(*refs, layers=layers, rows_n=rows_n, scale=scale)

    out = pl.pallas_call(
        run,
        out_shape=jax.ShapeDtypeStruct((layers, size, chans), jnp.float32),
        in_specs=[vmem] * layers,
        out_specs=vmem,
        scratch_shapes=[
            pltpu.VMEM((layers,) + shape[1:], jnp.bfloat16),
            pltpu.VMEM((layers,) + shape[1:], jnp.bfloat16),
            pltpu.VMEM((layers,) + shape[2:], jnp.bfloat16),
            pltpu.VMEM((layers,) + shape[2:], jnp.bfloat16),
            pltpu.VMEM((layers,) + shape[2:], jnp.bfloat16),
            dma((layers,)),
            dma((layers,)),
            dma((layers,)),
            dma((layers,)),
            dma((layers, rows_n)),
            dma((layers, rows_n)),
        ],
        compiler_params=pltpu.CompilerParams(collective_id=1, has_side_effects=True, vmem_limit_bytes=58 * 2**20),
    )(*terms)
    return out[:, : 27 * share].reshape(layers, 27, share * chans)


def spread_shares(term, chans, rows_n, cols_n):
    share = chans // (rows_n * cols_n)
    parts = term.reshape(27, rows_n, 2, 2, share, chans).transpose(3, 2, 1, 0, 4, 5)
    parts = parts.reshape(2, 2, rows_n, 27 * share, chans).astype(jnp.bfloat16)
    return jnp.pad(parts, ((0, 0), (0, 0), (0, 0), (0, -27 * share % 16), (0, 0)))


def body(inputs, upstream, kernels, norm_gain, norm_shift):
    frames, rows, width, chans = inputs.shape
    rows_n, cols_n = lax.axis_size("ha"), lax.axis_size("wa")
    total_rows, total_width = rows * rows_n, width * cols_n
    count = total_rows * total_width * chans
    scale = 1.0 / math.sqrt(frames * total_rows * total_width)
    layers = kernels.shape[0]
    a, w = lax.axis_index("ha"), lax.axis_index("wa")
    row_id = a * rows - 1 + jnp.arange(rows + 2)
    col_id = w * width - 8 + jnp.arange(width + 16)
    inside = ((row_id >= 0) & (row_id < total_rows))[:, None] & ((col_id >= 0) & (col_id < total_width))[None]
    mask = jnp.broadcast_to(inside[:, :, None].astype(jnp.float32), (rows + 2, width + 16, chans))
    plan, edge_rows = border_plan(frames, rows, width)
    f32, bf16 = jnp.float32, jnp.bfloat16
    own = ((frames, rows, width, chans), f32)
    stat_t = ((2 * frames, chans), f32)
    edge_t = ((edge_rows, chans), f32)
    wide_t = ((frames, rows + 2, width + 16, chans), f32)
    inv_t = ((frames, chans), f32)
    patch_t = ((frames * rows * width, 27 * chans), bf16)
    gains = [norm_gain[j : j + 1] for j in range(layers)]
    shifts = [norm_shift[j : j + 1] for j in range(layers)]

    up_plan = {key: (start + edge_rows, size) for key, (start, size) in plan.items()}
    values, up, stat, edges = call(
        lambda *r: start_kernel(*r, plan=plan, up_plan=up_plan),
        [inputs, upstream],
        [own, own, stat_t, ((2 * edge_rows, chans), f32)],
        [],
    )
    stream = values
    saved = []
    for layer in range(layers):
        if layer == 0:
            all_stat, border = exchange(stat, edges, [plan, up_plan], rows_n, cols_n, 2)
            up_stat, up_border = all_stat, border
        else:
            all_stat, border = exchange(stat, edges, [plan], rows_n, cols_n, 0)
        add = layer % 2 == 1 and layer < layers - 1
        conv = layer < layers - 1
        args = [values, border, all_stat, mask, kernels[layer], gains[layer], shifts[layer]]
        if add:
            args.append(stream)
        outs = [wide_t, inv_t, patch_t] + ([own, stat_t, edge_t] if conv else [])

        def run(*r, add=add, conv=conv):
            forward_kernel(*r, plan=plan, count=count, add=add, conv=conv)

        got = call(run, args, outs, [wide_t, ((3, frames + 2, rows + 2, width, chans), bf16)])
        saved.append(got[:3])
        if conv:
            values, stat, edges = got[3:]
            if add:
                stream = values

    terms, gain_sums, shift_sums = [None] * layers, [None] * layers, [None] * layers
    values = up
    grad_stream = None
    for layer in range(layers - 1, -1, -1):
        if layer == layers - 1:
            all_stat, border = up_stat, up_border
        else:
            all_stat, border = exchange(stat, edges, [plan], rows_n, cols_n, 0)
        args = [values, border, all_stat, mask, kernels[layer], gains[layer], shifts[layer], saved[layer][0], saved[layer][2]]
        normed_in = layer < layers - 1
        add = normed_in and layer % 2 == 1
        if normed_in:
            args += [saved[layer + 1][0], saved[layer + 1][1], gains[layer + 1]]
            total = jnp.sum(all_stat, axis=0)
            shift_sums[layer + 1] = jnp.sum(total[:frames], axis=0)
            gain_sums[layer + 1] = jnp.sum(total[frames:], axis=0)
        if add:
            args.append(grad_stream)

        from_plan = plan if normed_in else up_plan

        def run_back(*r, normed_in=normed_in, add=add, from_plan=from_plan):
            backward_kernel(*r, plan=plan, from_plan=from_plan, count=count, normed_in=normed_in, add=add)

        keep, term, values, stat, edges = call(
            run_back,
            args,
            [wide_t, ((27 * chans, chans), f32), own, stat_t, edge_t],
            [
                wide_t,
                ((3, frames + 4, rows + 2, width, chans), bf16),
                (((frames + 2) * rows * width, 27 * chans), bf16),
            ],
        )
        if layer % 2 == 1:
            grad_stream = keep
        terms[layer] = spread_shares(term, chans, rows_n, cols_n)
    all_stat, _ = exchange(stat, edges, [plan], rows_n, cols_n, 0)
    total = jnp.sum(all_stat, axis=0)
    shift_sums[0] = jnp.sum(total[:frames], axis=0)
    gain_sums[0] = jnp.sum(total[frames:], axis=0)
    s1 = (jnp.sum(total[:frames] * norm_gain[0], axis=1) / count)[:, None, None, None]
    s2 = (jnp.sum(total[frames:] * norm_gain[0], axis=1) / count)[:, None, None, None]
    cut = (slice(None), slice(1, rows + 1), slice(8, 8 + width))
    into = saved[0][1][:, None, None] * (values * norm_gain[0] - s1 - saved[0][0][cut] * s2)
    input_grad = (grad_stream[cut] + into).astype(jnp.bfloat16)
    norm_grads = jnp.stack([jnp.stack(gain_sums), jnp.stack(shift_sums)]) * scale
    kernel_grads = scatter_terms(terms, chans, rows_n, cols_n, scale)
    return (input_grad, kernel_grads, norm_grads)


def solution(mesh):
    return jax.shard_map(
        body,
        mesh=mesh,
        in_specs=(P("grp", "ha", "wa", None), P("grp", "ha", "wa", None), P(), P(), P()),
        out_specs=(P("grp", "ha", "wa", None), P("grp", None, ("ha", "wa")), P("grp", None, None)),
        check_vma=False,
    )
```
